128 devices in a mesh: row: 8 (over z, core), col: 16 (over x, y).
Axes of the slice: x: 4, y: 4, z: 4, core: 2. Of those that a mesh axis runs over, the one named last changes fastest.
Arguments:
- tensor_blocks: bfloat16 [128, 16, 4, 128, 128], P(None, 'row', None, 'col'), may hold values from -0.25 to 0.25
- density: bfloat16 [2048, 2048], P(('row', 'col')), may hold values from -6 to 6
- coef: bfloat16 [128, 16, 4, 128, 128], P('col'), may hold values from -0.03125 to 0.03125
- lam_list: int32 [16, 4], P('row'), may hold values from 0 to 15, all different within a row
- sig_list: int32 [16, 4], replicated, may hold values from 0 to 15, all different within a row
Outputs:
- exchange_matrix: float32 [2048, 2048], P('col', 'row')
The draws below stay inside these ranges and needn't reach their ends.
Inputs may be any that keep to these rules, and one draw needn't show every extreme that they name: `lam_list`: each row names 4 different tiles, and every tile is named by some row. `sig_list`: each row names 4 different tiles, and every tile is named by some row.
All inputs are finite; a program needn't handle non-finite values.
Results may differ from the reference program's by a relative error of at most 0.0029.
Values may be sent and summed in bfloat16 or wider, within the bound.
A program may use at most 128 MiB of HBM per device.

```python
import jax
import jax.numpy as jnp
from jax import lax

TILE = 128
NNZ = 4
NT = 16
NBAS = 2048
NAUX = 128


def with_spikes(values, stream_key, source, target, shards_of, factor):
    def block_of(axis_at):
        return (jnp.arange(values.shape[axis_at]) // (values.shape[axis_at] // shards_of)).reshape((-1,) + (1,) * (values.ndim - 1 - axis_at))

    near = jax.random.permutation(stream_key, shards_of)[block_of(target)]
    other_side = (block_of(target) + shards_of // 2) % shards_of
    return jnp.where((block_of(source) == near) | (block_of(source) == other_side), factor * values, values)


def levels(own_key, extent, split, least, top_value):
    loudness, own = 1.0, jax.random.fold_in(own_key, 6)
    for dim, blocks in split:
        heights = jnp.exp(jax.random.uniform(jax.random.fold_in(own, dim), (blocks,), jnp.float32, least / len(split), top_value / len(split)))
        loudness = loudness * jnp.repeat(heights, extent[dim] // blocks).reshape([-1 if axis == dim else 1 for axis in range(len(extent))])
    return loudness


def distinct(stream_key, rows, count, top, lift):
    order = jax.random.permutation(jax.random.fold_in(stream_key, 1), count)
    boost = order
    for power in range(3):
        boost = boost * boost // count
    boost = boost * lift // count
    lots = jax.random.randint(jax.random.fold_in(stream_key, 2), (rows, count), 0, 4096) + boost
    sure = jax.random.permutation(jax.random.fold_in(stream_key, 3), rows)[jnp.arange(count) % rows]
    lots = jnp.where(jnp.arange(rows)[:, None] == sure[None, :], 1 << 14, lots)
    score = lots * count + jnp.arange(count)
    return lax.top_k(score.astype(jnp.int32), top)[1].astype(jnp.int32)


def centred(rng, shape, spread, reach, cuts=(), held_as=jnp.bfloat16):
    values = jax.random.normal(rng, shape, jnp.float32) * spread
    if len(cuts) > 0:
        values = levels(rng, shape, cuts, -0.22, 0.18) * values
    return jnp.clip(values, min=-reach, max=reach).astype(held_as)


def bell_draw_with(own_key, dims, scale, most, shards, heavy, held_as=jnp.bfloat16):
    array = scale * jax.random.normal(own_key, dims, jnp.float32)
    if shards:
        array = array * levels(own_key, dims, shards, -0.22, 0.18)
    return jnp.clip(with_spikes(array, jax.random.fold_in(own_key, 3), *heavy), -most, most).astype(held_as)


def setup_inputs(seed: int = 0) -> dict:
    seeds = jax.random.split(jax.random.key(seed), 6)
    tensor_blocks = centred(seeds[0], (NAUX, NT, NNZ, TILE, TILE), (NNZ * TILE) ** -0.5, 0.25, ((1, 8), (3, 16)))
    density = centred(seeds[1], (NBAS, NBAS), 1.0, 6.0, ((0, 128),))
    coef = bell_draw_with(seeds[2], (NAUX, NT, NNZ, TILE, TILE), (NAUX * NNZ * TILE) ** -0.5, 0.03125, ((0, 16),), (0, 1, 16, 2.0))
    lam_list = distinct(seeds[3], NT, NT, NNZ, 0)
    sig_list = distinct(seeds[4], NT, NT, NNZ, 0)
    return {"tensor_blocks": tensor_blocks, "density": density, "coef": coef, "lam_list": lam_list, "sig_list": sig_list}


def reference(tensor_blocks, density, coef, lam_list, sig_list):
    density_tiles = density.reshape(NT, TILE, NBAS)

    def one_mu(mu_tile):
        blocks = tensor_blocks[:, mu_tile]
        tile_rows = density_tiles[lam_list[mu_tile]]
        products = jnp.einsum("akij,kjn->ain", blocks.astype(jnp.float32), tile_rows.astype(jnp.float32)).astype(jnp.bfloat16)
        by_tile = products.reshape(NAUX, TILE, NT, TILE)

        def one_nu(nu_tile):
            picked = jnp.take(by_tile, sig_list[nu_tile], axis=2)
            return jnp.einsum("amkj,akij->im", picked.astype(jnp.float32), coef[:, nu_tile].astype(jnp.float32))

        return lax.map(one_nu, jnp.arange(NT, dtype=jnp.int32))

    stacked = lax.map(one_mu, jnp.arange(NT, dtype=jnp.int32))
    return stacked.transpose(1, 2, 0, 3).reshape(NBAS, NBAS)
```

```python
import jax
import jax.numpy as jnp
from jax import lax
from jax.sharding import PartitionSpec as P


def per_device(tensor_blocks, density, coef, lam_list, sig_list):
    gathered = lax.all_gather(density, ("row", "col"), axis=0, tiled=True)
    basis_count = gathered.shape[0]
    tile_width = tensor_blocks.shape[-1]
    tile_count = basis_count // tile_width
    tile_rows = gathered.reshape(tile_count, tile_width, basis_count)[lam_list]
    blocks = lax.all_to_all(tensor_blocks, "col", split_axis=0, concat_axis=3, tiled=True)
    products = jnp.einsum("atkij,tkjn->atin", blocks, tile_rows, preferred_element_type=jnp.float32).astype(jnp.bfloat16)
    aux_count = products.shape[0]
    mu_rows = products.shape[1] * products.shape[2]
    by_tile = products.reshape(aux_count, mu_rows, tile_count, tile_width)
    picked = jnp.take(by_tile, sig_list, axis=2)
    partial_sum = jnp.einsum("amukj,aukij->uim", picked, coef, preferred_element_type=jnp.float32)
    return lax.psum_scatter(partial_sum.reshape(basis_count, mu_rows), "col", scatter_dimension=0, tiled=True)


def solution(mesh):
    in_specs = (
        P(None, "row", None, "col", None),
        P(("row", "col"), None),
        P("col", None, None, None, None),
        P("row", None),
        P(),
    )
    return jax.shard_map(per_device, mesh=mesh, in_specs=in_specs, out_specs=P("col", "row"), check_vma=False)
```

```python
import functools

import jax
import jax.numpy as jnp
from jax import lax
from jax.experimental import pallas as pl
from jax.experimental.pallas import tpu as pltpu
from jax.sharding import PartitionSpec as P

MESH = pl.DeviceIdType.MESH
F32, BF16 = jnp.float32, jnp.bfloat16
OPT = dict(D=True, T=True, S1=True, S2=True, K=True, groups=2, parts=((0, 512), (512, 512), (1024, 1024)), t_late=False)
ORDERS = (("y", "z", "x"), ("z", "x", "y"), ("x", "y", "z"))


def kernel(opt, lam_ref, sig_ref, t_hbm, d_hbm, c_hbm, out_ref, dbuf, cbuf, rbuf, tl, prod, kacc, kbf, krecv,
           d_send, d_recv, t_send, t_recv, k_send, k_recv, loc_sem, c_sem):
    groups = opt["groups"]
    pg = 8 // groups
    r, c = lax.axis_index("row"), lax.axis_index("col")
    z, core, x, y = r // 2, r % 2, c // 4, c % 4
    here = {"x": x, "y": y, "z": z}

    def peer(axis, step):
        n = lax.rem(here[axis] + step + 4, 4)
        if axis == "z":
            return (n * 2 + core, c)
        return (r, n * 4 + y) if axis == "x" else (r, x * 4 + n)

    sibling = (r + 1 - 2 * core, c)

    for p in range(8):
        pltpu.make_async_copy(c_hbm.at[p], cbuf.at[p], c_sem.at[p]).start()
    own_d = pltpu.make_async_copy(d_hbm, dbuf.at[z, core, x, y], loc_sem.at[0])
    own_d.start()
    own_t = pltpu.make_async_copy(t_hbm.at[pl.ds(c * 8, 8)], rbuf.at[c], loc_sem.at[1])
    own_t.start()

    barrier = pltpu.get_barrier_semaphore()

    @pl.loop(1, 16)
    def _(i):
        pl.semaphore_signal(barrier, inc=1, device_id=(r, lax.rem(c + i, 16)), device_id_type=MESH)

    for dev in (peer("z", 1), peer("z", -1), sibling):
        pl.semaphore_signal(barrier, inc=1, device_id=dev, device_id_type=MESH)
    pl.semaphore_wait(barrier, 18)

    def t_copy(g, dst, src):
        return pltpu.make_async_remote_copy(
            src_ref=t_hbm.at[pl.ds(dst * 8 + g * pg, pg)], dst_ref=rbuf.at[src, pl.ds(g * pg, pg)],
            send_sem=t_send.at[g, dst], recv_sem=t_recv.at[g, src], device_id=(r, dst), device_id_type=MESH)

    def t_start():
        for g in range(groups):
            @pl.loop(1, 16)
            def _(i):
                t_copy(g, lax.rem(c + i, 16), c).start()

    own_d.wait()

    def region(part, done, at, core_at, sub=None):
        first, width = opt["parts"][part]
        if sub is not None:
            half = (width // 256) * 128
            first, width = (first, half) if sub == 0 else (first + half, width - half)
        pos = {a: (slice(None) if a in done else at.get(a, here[a])) for a in "xyz"}
        return dbuf.at[pos["z"], core_at, pos["x"], pos["y"], :, pl.ds(first, width)]

    def d_copy(ref, s, dev):
        return pltpu.make_async_remote_copy(src_ref=ref, dst_ref=ref, send_sem=d_send.at[s], recv_sem=d_recv.at[s],
                                            device_id=dev, device_id_type=MESH)

    started = []
    sib_wait = []

    def wait_recv(ref, s):
        pltpu.make_async_copy(ref, ref, d_recv.at[s]).wait()

    def to_sibling(part, done, at, sub, s):
        cp = d_copy(region(part, done, at, core, sub), s, sibling)
        cp.start()
        started.append(cp)
        sib_wait.append((region(part, done, at, 1 - core, sub), s))

    if opt["D"]:
        if not opt["t_late"] and opt["T"]:
            t_start()
        nparts = range(len(opt["parts"]))
        for phase in range(3):
            for p in nparts:
                done, axis = ORDERS[p][:phase], ORDERS[p][phase]
                base = p * 17 + phase * 4
                for j, step in enumerate((1, -1)):
                    cp = d_copy(region(p, done, {}, core), base + j, peer(axis, step))
                    cp.start()
                    started.append(cp)
            if phase == 2:
                for p in nparts:
                    to_sibling(p, ORDERS[p][:phase], {}, None, p * 17 + 12)
            for p in nparts:
                done, axis = ORDERS[p][:phase], ORDERS[p][phase]
                base = p * 17 + phase * 4
                for j, step in enumerate((1, -1)):
                    at = {axis: lax.rem(here[axis] - step + 4, 4)}
                    wait_recv(region(p, done, at, core), base + j)
                    cp = d_copy(region(p, done, at, core, j), base + 2 + j, peer(axis, step))
                    cp.start()
                    started.append(cp)
                    if phase == 2:
                        to_sibling(p, done, at, None, p * 17 + 13 + j)
            for p in nparts:
                done, axis = ORDERS[p][:phase], ORDERS[p][phase]
                base = p * 17 + phase * 4
                for j in range(2):
                    at = {axis: lax.rem(here[axis] + 2, 4)}
                    wait_recv(region(p, done, at, core, j), base + 2 + j)
                    if phase == 2:
                        to_sibling(p, done, at, j, p * 17 + 15 + j)
        if opt["t_late"] and opt["T"]:
            t_start()
        for ref, s in sib_wait:
            wait_recv(ref, s)
    elif opt["T"]:
        t_start()
    own_t.wait()

    for g in range(groups):
        if opt["T"]:
            @pl.loop(1, 16)
            def _(i):
                t_copy(g, c, lax.rem(c + i, 16)).wait_recv()
        if opt["S1"]:
            for t in range(2):
                for p in range(g * pg, (g + 1) * pg):
                    for kk in range(2):
                        both = rbuf[:, p, (t * 2 + kk) * 16:(t * 2 + kk + 1) * 16, :].astype(F32).reshape(16, 2, 8, 128)
                        for h in range(2):
                            tl[t, pl.ds((p - g * pg) * 128, 128), pl.ds((kk * 2 + h) * 128, 128)] = both[:, h].reshape(128, 128).astype(BF16)
            for t in range(2):
                lams = [lam_ref[t, k] for k in range(4)]

                @pl.loop(0, 2048 // opt.get("ncol", 256))
                def _(n):
                    nc = opt.get("ncol", 256)
                    cols = pl.ds(pl.multiple_of(n * nc, nc), nc)
                    rhs = jnp.concatenate(
                        [dbuf[lam // 4, (lam // 2) % 2, pl.ds((lam % 2) * 2, 2), :, :, cols].reshape(128, nc) for lam in lams], axis=0)
                    res = jnp.dot(tl[t], rhs, preferred_element_type=F32).astype(BF16)
                    for p in range(pg):
                        for h in range(nc // 128):
                            prod[g * pg + p, n * (nc // 128) + h, pl.ds(t * 128, 128), :] = res[p * 128:(p + 1) * 128, h * 128:(h + 1) * 128]
        for p in range(g * pg, (g + 1) * pg):
            pltpu.make_async_copy(c_hbm.at[p], cbuf.at[p], c_sem.at[p]).wait()

        @pl.loop(1, 17)
        def _(i):
            nu = lax.rem(c + i, 16)
            if opt["S2"]:
                sigs = [sig_ref[k, nu] for k in range(4)]
                lhs = jnp.concatenate([cbuf[p, nu, k] for p in range(g * pg, (g + 1) * pg) for k in range(4)], axis=1)
                rhs = jnp.concatenate([prod[p, s] for p in range(g * pg, (g + 1) * pg) for s in sigs], axis=1)
                acc = lax.dot_general(lhs, rhs, (((1,), (1,)), ((), ())), preferred_element_type=F32)
                if g > 0:
                    acc += kacc[nu]
                if g < groups - 1:
                    kacc[nu] = acc
            if g == groups - 1:
                if opt["S2"]:
                    kbf[nu] = acc.astype(BF16)
                if opt["K"]:
                    @pl.when(nu != c)
                    def _():
                        pltpu.make_async_remote_copy(
                            src_ref=kbf.at[nu], dst_ref=krecv.at[c], send_sem=k_send.at[nu], recv_sem=k_recv.at[c],
                            device_id=(r, nu), device_id_type=MESH).start()

                    @pl.when(nu == c)
                    def _():
                        out_ref[...] = acc if opt["S2"] else jnp.zeros_like(out_ref)

    if opt["K"]:
        @pl.loop(1, 16)
        def _(i):
            src = lax.rem(c + i, 16)
            pltpu.make_async_remote_copy(
                src_ref=kbf.at[src], dst_ref=krecv.at[src], send_sem=k_send.at[src], recv_sem=k_recv.at[src],
                device_id=(r, src), device_id_type=MESH).wait_recv()
            out_ref[...] += krecv[src].astype(F32)

        @pl.loop(1, 16)
        def _(i):
            dst = lax.rem(c + i, 16)
            pltpu.make_async_remote_copy(
                src_ref=kbf.at[dst], dst_ref=krecv.at[c], send_sem=k_send.at[dst], recv_sem=k_recv.at[c],
                device_id=(r, dst), device_id_type=MESH).wait_send()
    else:
        out_ref[...] = kacc[0]
    for cp in started:
        cp.wait_send()
    if opt["T"]:
        for g in range(groups):
            @pl.loop(1, 16)
            def _(i):
                t_copy(g, lax.rem(c + i, 16), c).wait_send()


def per_device(opt, tensor_blocks, density, coef, lam_list, sig_list):
    groups = opt["groups"]
    pg = 8 // groups
    return pl.pallas_call(
        functools.partial(kernel, opt),
        out_shape=jax.ShapeDtypeStruct((128, 256), F32),
        in_specs=[pl.BlockSpec(memory_space=pltpu.SMEM)] * 2 + [pl.BlockSpec(memory_space=pl.ANY)] * 3,
        out_specs=pl.BlockSpec(memory_space=pltpu.VMEM),
        scratch_shapes=[
            pltpu.VMEM((4, 2, 4, 4, 16, 2048), BF16),
            pltpu.VMEM((8, 16, 4, 128, 128), BF16),
            pltpu.VMEM((16, 8, 64, 128), BF16),
            pltpu.VMEM((2, pg * 128, 512), BF16),
            pltpu.VMEM((8, 16, 256, 128), BF16),
            pltpu.VMEM((16, 128, 256), F32),
            pltpu.VMEM((16, 128, 256), BF16),
            pltpu.VMEM((16, 128, 256), BF16),
            pltpu.SemaphoreType.DMA((51,)),
            pltpu.SemaphoreType.DMA((51,)),
            pltpu.SemaphoreType.DMA((groups, 16)),
            pltpu.SemaphoreType.DMA((groups, 16)),
            pltpu.SemaphoreType.DMA((16,)),
            pltpu.SemaphoreType.DMA((16,)),
            pltpu.SemaphoreType.DMA((2,)),
            pltpu.SemaphoreType.DMA((8,)),
        ],
        compiler_params=pltpu.CompilerParams(collective_id=0, has_side_effects=True, vmem_limit_bytes=60 * 2**20),
        cost_estimate=pl.CostEstimate(flops=2**33, bytes_accessed=20 * 2**20, transcendentals=0),
    )(lam_list, sig_list.T, tensor_blocks.reshape(128, 64, 128), density, coef)


def solution(mesh, **kw):
    in_specs = (
        P(None, "row", None, "col", None),
        P(("row", "col"), None),
        P("col", None, None, None, None),
        P("row", None),
        P(),
    )
    return jax.shard_map(functools.partial(per_device, {**OPT, **kw}), mesh=mesh, in_specs=in_specs, out_specs=P("col", "row"), check_vma=False)
```

```python
import functools

import jax
import jax.numpy as jnp
from jax import lax
from jax.experimental import pallas as pl
from jax.experimental.pallas import tpu as pltpu
from jax.sharding import PartitionSpec as P

MESH = pl.DeviceIdType.MESH
F32, BF16 = jnp.float32, jnp.bfloat16
PARTS = (("xyz", 0, 768), ("yxz", 768, 768), ("zxy", 1536, 256), ("zyx", 1792, 256))
ORDER = tuple(((i + i // 4) % 4, i % 4) for i in range(1, 16))
SCHED = (("1", 0), ("1", 1), ("1", 2), ("1", 3), ("1b", 0), ("1b", 1), ("1b", 2), ("1b", 3), ("T", 0, 2), ("2", 0), ("2", 1), ("2", 2), ("2", 3),
         ("T", 2, 4), ("C",), ("3", 2), ("3", 3), ("T", 4, 8), ("3", 0), ("3", 1), ("4", 2), ("4", 3), ("4", 0), ("4", 1), ("S",))
OPT = dict(S1=True, S2=True, K=True, pg=4, parts=PARTS, sched=SCHED, order=ORDER, bar=False, mid=13)


def kernel(opt, lam_ref, sig_ref, t_hbm, d_hbm, c_hbm, out_ref, cbuf, rbuf, tl, prod, kbf, krecv,
           d_send, d_recv, t_send, t_recv, k_send, k_recv, loc_sem, c_sem, kmid, ksum, m_recv, *dparts):
    parts, pg = opt["parts"], opt["pg"]
    r, c = lax.axis_index("row"), lax.axis_index("col")
    z, core, x, y = r // 2, r % 2, c // 4, c % 4
    here = {"x": x, "y": y, "z": z}

    def peer(axis, step):
        n = lax.rem(here[axis] + step + 4, 4)
        if axis == "z":
            return (n * 2 + core, c)
        return (r, n * 4 + y) if axis == "x" else (r, x * 4 + n)

    sibling = (r + 1 - 2 * core, c)

    own_d = [pltpu.make_async_copy(d_hbm.at[:, pl.ds(first, width)],
                                   dparts[p].at[here[order[2]], core, here[order[1]], here[order[0]]], loc_sem.at[p])
             for p, (order, first, width) in enumerate(parts)]
    for cp in own_d:
        cp.start()
    for p in range(8):
        pltpu.make_async_copy(t_hbm.at[c * 8 + p], rbuf.at[c, p], t_recv.at[p]).start()

    barrier = pltpu.get_barrier_semaphore()

    def greet(dev):
        pl.semaphore_signal(barrier, inc=1, device_id=dev, device_id_type=MESH)

    for axis in "xyz":
        for step in (1, 2, 3):
            greet(peer(axis, step))
    greet(sibling)
    if opt["bar"]:
        for dx in (1, 2, 3):
            for dy in (1, 2, 3):
                greet((r, lax.rem(x + dx, 4) * 4 + lax.rem(y + dy, 4)))
    pl.semaphore_wait(barrier, 19 if opt["bar"] else 10)

    def t_start(first, last):
        @pl.loop(first, last)
        def _(p):
            for dx, dy in opt["order"]:
                dst = lax.rem(x + dx, 4) * 4 + lax.rem(y + dy, 4)
                pltpu.make_async_remote_copy(src_ref=t_hbm.at[dst * 8 + p], dst_ref=rbuf.at[c, p], send_sem=t_send.at[p], recv_sem=t_recv.at[p],
                                             device_id=(r, dst), device_id_type=MESH).start()

    started = []
    sib_wait = {p: [] for p in range(len(parts))}
    NS = 16

    def d_start(ref, s, dev):
        cp = pltpu.make_async_remote_copy(src_ref=ref, dst_ref=ref, send_sem=d_send.at[s], recv_sem=d_recv.at[s],
                                          device_id=dev, device_id_type=MESH)
        cp.start()
        started.append(cp)

    def d_wait(ref, s):
        pltpu.make_async_copy(ref, ref, d_recv.at[s]).wait()

    def shifted(axis, step):
        return lax.rem(here[axis] + step + 4, 4)

    def level1(p, a, core_at=core):
        o = parts[p][0]
        return dparts[p].at[here[o[2]], core_at, here[o[1]], a]

    def level2(p, a):
        o = parts[p][0]
        return dparts[p].at[here[o[2]], core, a]

    def level3(p, a, core_at, half=None):
        ref = dparts[p].at[a, core_at]
        return ref if half is None else ref.at[pl.ds(half * 2, 2)]

    def to_sibling(p, a, half, j):
        d_start(level3(p, a, core, half), p * NS + 4 + j, sibling)
        sib_wait[p].append((level3(p, a, 1 - core, half), p * NS + 4 + j))

    STEPS = (1, -1, 2)
    ps = range(len(parts))

    def stage1(p):
        o, first, width = parts[p]
        for j, step in enumerate(STEPS):
            s = p * NS + 10 + j
            cp = pltpu.make_async_remote_copy(src_ref=d_hbm.at[:, pl.ds(first, width)], dst_ref=level1(p, here[o[0]]), send_sem=d_send.at[s],
                                              recv_sem=d_recv.at[s], device_id=peer(o[0], step), device_id_type=MESH)
            cp.start()
            started.append(cp)

    def stage1b(p):
        o = parts[p][0]
        own_d[p].wait()
        for j, step in enumerate(STEPS):
            d_wait(level1(p, shifted(o[0], -step)), p * NS + 10 + j)
        for j, step in enumerate(STEPS):
            d_start(level2(p, here[o[1]]), p * NS + 13 + j, peer(o[1], step))

    def stage2(p):
        o = parts[p][0]
        for j, step in enumerate(STEPS):
            d_wait(level2(p, shifted(o[1], -step)), p * NS + 13 + j)
        for j, step in enumerate((1, -1)):
            d_start(level3(p, here[o[2]], core), p * NS + j, peer(o[2], step))
        to_sibling(p, here[o[2]], None, 0)

    def stage3(p):
        o = parts[p][0]
        for j, step in enumerate((1, -1)):
            at = shifted(o[2], -step)
            d_wait(level3(p, at, core), p * NS + j)
            d_start(level3(p, at, core, j), p * NS + 2 + j, peer(o[2], step))
            to_sibling(p, at, None, 1 + j)

    def stage4(p):
        o = parts[p][0]
        for j in range(2):
            at = shifted(o[2], 2)
            d_wait(level3(p, at, core, j), p * NS + 2 + j)
            to_sibling(p, at, j, 3 + j)

    def c_start():
        for p in range(8):
            pltpu.make_async_copy(c_hbm.at[p], cbuf.at[p], c_sem.at[p]).start()

    def t_gather(p):
        pltpu.make_async_copy(rbuf.at[:, p], rbuf.at[:, p], t_recv.at[p]).wait()
        if opt["S1"]:
            for t in range(2):
                for kk in range(2):
                    both = rbuf[:, p, (t * 2 + kk) * 16:(t * 2 + kk + 1) * 16, :].astype(F32).reshape(16, 2, 8, 128)
                    for h in range(2):
                        tl[t, pl.ds(pl.multiple_of(p * 128, 128), 128), pl.ds((kk * 2 + h) * 128, 128)] = both[:, h].reshape(128, 128).astype(BF16)

    def lam_rows(p, lam, cols):
        o = parts[p][0]
        pos = {"z": lam // 4, "x": pl.ds(lax.rem(lam, 2) * 2, 2), "y": slice(None)}
        v = dparts[p][pos[o[2]], lax.rem(lam // 2, 2), pos[o[1]], pos[o[0]], :, cols]
        if o.index("y") > o.index("x"):
            v = jnp.swapaxes(v, 0, 1)
        return v.reshape(128, v.shape[-1])

    def step1():
        for p in ps:
            while sib_wait[p]:
                d_wait(*sib_wait[p].pop(0))

        @pl.loop(0, 8 // pg)
        def _(g):
            for q in range(pg):
                t_gather(g * pg + q)
            if not opt["S1"]:
                return

            for t in range(2):
                lams = [lam_ref[t, k] for k in range(4)]
                lhs = tl[t, pl.ds(pl.multiple_of(g * pg * 128, pg * 128), pg * 128)]
                for p in ps:
                    _, first, width = parts[p]
                    for start in range(0, width, 512):
                        nc = min(512, width - start)
                        rhs = jnp.concatenate([lam_rows(p, lam, pl.ds(start, nc)) for lam in lams], axis=0)
                        res = jnp.dot(lhs, rhs, preferred_element_type=F32).astype(BF16)
                        for q in range(pg):
                            for h in range(nc // 128):
                                prod[g * pg + q, (first + start) // 128 + h, :, pl.ds(t * 128, 128)] = (
                                    res[q * 128:(q + 1) * 128, h * 128:(h + 1) * 128].T)

    acts = {"1": stage1, "1b": stage1b, "2": stage2, "3": stage3, "4": stage4, "T": t_start, "S": step1, "C": c_start}
    used = set(opt["sched"])
    for name, *arg in opt["sched"]:
        acts[name](*arg)
    for p in ps:
        if ("1b", p) not in used:
            own_d[p].wait()
    if ("C",) in used:
        for p in range(8):
            pltpu.make_async_copy(c_hbm.at[p], cbuf.at[p], c_sem.at[p]).wait()

    def step2(nu):
        if not opt["S2"]:
            return jnp.zeros((128, 256), F32)
        sigs = [sig_ref[k, nu] for k in range(4)]
        lhs = jnp.concatenate([cbuf[p, nu, k] for p in range(8) for k in range(4)], axis=1)
        rhs = jnp.concatenate([prod[p, s] for p in range(8) for s in sigs], axis=0)
        return jnp.dot(lhs, rhs, preferred_element_type=F32)

    def spot(dx, dy):
        return lax.rem(x + dx + 4, 4) * 4 + lax.rem(y + dy + 4, 4)

    def mid_copy(s, nu, slot, dst):
        return pltpu.make_async_remote_copy(src_ref=kbf.at[nu], dst_ref=kmid.at[slot], send_sem=k_send.at[s], recv_sem=m_recv.at[slot],
                                            device_id=(r, dst), device_id_type=MESH)

    def own_copy(src_ref, s, dst, src):
        return pltpu.make_async_remote_copy(src_ref=src_ref, dst_ref=krecv.at[src], send_sem=k_send.at[s], recv_sem=k_recv.at[src],
                                            device_id=(r, dst), device_id_type=MESH)

    FIRST = 7

    def send(i, dx, dy, nu):
        @pl.when((i < 4) & (dx != 0))
        def _():
            mid_copy(i, nu, dx - 1, spot(dx, 0)).start()

        @pl.when((i >= 4) & (i < FIRST) & (dy != 0))
        def _():
            mid_copy(i, nu, 3 + dy // 2, spot(0, dy)).start()

        @pl.when((i >= FIRST) & (i < 15))
        def _():
            own_copy(kbf.at[nu], i, nu, c).start()

        @pl.when(i == opt["mid"])
        def _():
            for slot in range(5):
                pltpu.make_async_copy(kmid.at[slot], kmid.at[slot], m_recv.at[slot]).wait()
            for j, (slots, at) in enumerate((((0, 1, 2), spot(0, 2)), ((3, 4), spot(2, 0)))):
                tot = kbf[at].astype(F32)
                for slot in slots:
                    tot += kmid[slot].astype(F32)
                ksum[j] = tot.astype(BF16)
                own_copy(ksum.at[j], 16 + j, at, c).start()

    def two_nus(i, carry):
        cx, cy = carry
        at = [(cx % 4, cy % 4), (cx // 4 % 4, cy // 4 % 4)]
        nus = [spot(*v) for v in at]
        accs = [step2(nu) for nu in nus]
        for nu, acc in zip(nus, accs):
            kbf[nu] = acc.astype(BF16)
        if opt["K"]:
            for j in range(2):
                send(2 * i + j, *at[j], nus[j])

        @pl.when(i == 7)
        def _():
            out_ref[...] = accs[1]

        return cx // 16, cy // 16

    SEQ = ((1, 2), (2, 2), (3, 2), (0, 2), (2, 1), (2, 3), (2, 0), (1, 1), (3, 3), (1, 3), (3, 1), (1, 0), (0, 1), (3, 0), (0, 3))
    lax.fori_loop(0, 8, two_nus, tuple(jnp.int32(sum(v[a] * 4**i for i, v in enumerate(SEQ))) for a in range(2)))

    for cp in started:
        cp.wait_send()
    for p in range(8):
        if any(u[0] == "T" for u in used):
            pltpu.make_async_copy(rbuf.at[pl.ds(0, 15), p], rbuf.at[pl.ds(0, 15), p], t_send.at[p]).wait()

    if opt["K"]:
        last = SEQ[FIRST:] + ((0, 2), (2, 0))
        for dx, dy in last:
            src = spot(-dx, -dy)
            own_copy(ksum.at[0], 0, c, src).wait_recv()
            out_ref[...] += krecv[src].astype(F32)
        for i, (dx, dy) in enumerate(SEQ):
            if (dx, dy) not in ((0, 2), (2, 0)):
                pltpu.make_async_copy(kbf.at[0], kbf.at[0], k_send.at[i]).wait()
        for j in range(2):
            pltpu.make_async_copy(kbf.at[0], kbf.at[0], k_send.at[16 + j]).wait()


def per_device(opt, tensor_blocks, density, coef, lam_list, sig_list):
    parts = opt["parts"]
    return pl.pallas_call(
        functools.partial(kernel, opt),
        out_shape=jax.ShapeDtypeStruct((128, 256), F32),
        in_specs=[pl.BlockSpec(memory_space=pltpu.SMEM)] * 2 + [pl.BlockSpec(memory_space=pl.ANY)] * 3,
        out_specs=pl.BlockSpec(memory_space=pltpu.VMEM),
        scratch_shapes=[
            pltpu.VMEM((8, 16, 4, 128, 128), BF16),
            pltpu.VMEM((16, 8, 64, 128), BF16),
            pltpu.VMEM((2, 1024, 512), BF16),
            pltpu.VMEM((8, 16, 128, 256), BF16),
            pltpu.VMEM((16, 128, 256), BF16),
            pltpu.VMEM((16, 128, 256), BF16),
            pltpu.SemaphoreType.DMA((16 * len(parts),)),
            pltpu.SemaphoreType.DMA((16 * len(parts),)),
            pltpu.SemaphoreType.DMA((8,)),
            pltpu.SemaphoreType.DMA((8,)),
            pltpu.SemaphoreType.DMA((18,)),
            pltpu.SemaphoreType.DMA((16,)),
            pltpu.SemaphoreType.DMA((len(parts),)),
            pltpu.SemaphoreType.DMA((8,)),
            pltpu.VMEM((5, 128, 256), BF16),
            pltpu.VMEM((2, 128, 256), BF16),
            pltpu.SemaphoreType.DMA((5,)),
        ] + [pltpu.VMEM((4, 2, 4, 4, 16, width), BF16) for _, _, width in parts],
        compiler_params=pltpu.CompilerParams(collective_id=0, has_side_effects=True, vmem_limit_bytes=60 * 2**20),
        cost_estimate=pl.CostEstimate(flops=2**33, bytes_accessed=20 * 2**20, transcendentals=0),
    )(lam_list, sig_list.T, tensor_blocks.reshape(128, 64, 128), density, coef)


def solution(mesh, **kw):
    in_specs = (
        P(None, "row", None, "col", None),
        P(("row", "col"), None),
        P("col", None, None, None, None),
        P("row", None),
        P(),
    )
    return jax.shard_map(functools.partial(per_device, {**OPT, **kw}), mesh=mesh, in_specs=in_specs, out_specs=P("col", "row"), check_vma=False)
```

```python
import functools

import jax
import jax.numpy as jnp
from jax import lax
from jax.experimental import pallas as pl
from jax.experimental.pallas import tpu as pltpu
from jax.sharding import PartitionSpec as P

MESH = pl.DeviceIdType.MESH
F32, BF16 = jnp.float32, jnp.bfloat16
PARTS = (("xyz", 0, 768), ("yxz", 768, 768), ("zxy", 1536, 256), ("zyx", 1792, 256))
ORDER = tuple(((i + i // 4) % 4, i % 4) for i in range(1, 16))
SCHED = (("1", 0), ("1", 1), ("1", 2), ("1", 3), ("1b", 0), ("1b", 1), ("1b", 2), ("1b", 3), ("T", 0, 2), ("2", 0), ("2", 1), ("2", 2), ("2", 3),
         ("T", 2, 4), ("C",), ("3", 2), ("3", 3), ("T", 4, 8), ("3", 0), ("3", 1), ("4", 2), ("4", 3), ("4", 0), ("4", 1), ("S",))
OPT = dict(S1=True, S2=True, K=True, pg=4, parts=PARTS, sched=SCHED, order=ORDER, bar=False, mid=13)


def kernel(opt, lam_ref, sig_ref, t_hbm, d_hbm, c_hbm, out_ref, cbuf, rbuf, tl, prod, kbf, krecv,
           d_send, d_recv, t_send, t_recv, k_send, k_recv, loc_sem, c_sem, kmid, ksum, m_recv, *dparts):
    parts, pg = opt["parts"], opt["pg"]
    r, c = lax.axis_index("row"), lax.axis_index("col")
    z, core, x, y = r // 2, r % 2, c // 4, c % 4
    here = {"x": x, "y": y, "z": z}

    def peer(axis, step):
        n = lax.rem(here[axis] + step + 4, 4)
        if axis == "z":
            return (n * 2 + core, c)
        return (r, n * 4 + y) if axis == "x" else (r, x * 4 + n)

    sibling = (r + 1 - 2 * core, c)

    own_d = [pltpu.make_async_copy(d_hbm.at[:, pl.ds(first, width)],
                                   dparts[p].at[here[order[2]], core, here[order[1]], here[order[0]]], loc_sem.at[p])
             for p, (order, first, width) in enumerate(parts)]
    for cp in own_d:
        cp.start()
    for p in range(8):
        pltpu.make_async_copy(t_hbm.at[c * 8 + p], rbuf.at[c, p], t_recv.at[p]).start()

    barrier = pltpu.get_barrier_semaphore()

    def greet(dev):
        pl.semaphore_signal(barrier, inc=1, device_id=dev, device_id_type=MESH)

    for axis in "xyz":
        for step in (1, 2, 3):
            greet(peer(axis, step))
    greet(sibling)
    if opt["bar"]:
        for dx in (1, 2, 3):
            for dy in (1, 2, 3):
                greet((r, lax.rem(x + dx, 4) * 4 + lax.rem(y + dy, 4)))
    pl.semaphore_wait(barrier, 19 if opt["bar"] else 10)

    def t_start(first, last):
        @pl.loop(first, last)
        def _(p):
            for dx, dy in opt["order"]:
                dst = lax.rem(x + dx, 4) * 4 + lax.rem(y + dy, 4)
                pltpu.make_async_remote_copy(src_ref=t_hbm.at[dst * 8 + p], dst_ref=rbuf.at[c, p], send_sem=t_send.at[p], recv_sem=t_recv.at[p],
                                             device_id=(r, dst), device_id_type=MESH).start()

    started = []
    sib_wait = {p: [] for p in range(len(parts))}
    NS = 16

    def d_start(ref, s, dev):
        cp = pltpu.make_async_remote_copy(src_ref=ref, dst_ref=ref, send_sem=d_send.at[s], recv_sem=d_recv.at[s],
                                          device_id=dev, device_id_type=MESH)
        cp.start()
        started.append(cp)

    def d_wait(ref, s):
        pltpu.make_async_copy(ref, ref, d_recv.at[s]).wait()

    def shifted(axis, step):
        return lax.rem(here[axis] + step + 4, 4)

    def level1(p, a, core_at=core):
        o = parts[p][0]
        return dparts[p].at[here[o[2]], core_at, here[o[1]], a]

    def level2(p, a):
        o = parts[p][0]
        return dparts[p].at[here[o[2]], core, a]

    def level3(p, a, core_at, half=None):
        ref = dparts[p].at[a, core_at]
        return ref if half is None else ref.at[pl.ds(half * 2, 2)]

    def to_sibling(p, a, half, j):
        d_start(level3(p, a, core, half), p * NS + 4 + j, sibling)
        sib_wait[p].append((level3(p, a, 1 - core, half), p * NS + 4 + j))

    STEPS = (1, -1, 2)
    ps = range(len(parts))

    def stage1(p):
        o, first, width = parts[p]
        for j, step in enumerate(STEPS):
            s = p * NS + 10 + j
            cp = pltpu.make_async_remote_copy(src_ref=d_hbm.at[:, pl.ds(first, width)], dst_ref=level1(p, here[o[0]]), send_sem=d_send.at[s],
                                              recv_sem=d_recv.at[s], device_id=peer(o[0], step), device_id_type=MESH)
            cp.start()
            started.append(cp)

    def stage1b(p):
        o = parts[p][0]
        own_d[p].wait()
        for j, step in enumerate(STEPS):
            d_wait(level1(p, shifted(o[0], -step)), p * NS + 10 + j)
        for j, step in enumerate(STEPS):
            d_start(level2(p, here[o[1]]), p * NS + 13 + j, peer(o[1], step))

    def stage2(p):
        o = parts[p][0]
        for j, step in enumerate(STEPS):
            d_wait(level2(p, shifted(o[1], -step)), p * NS + 13 + j)
        for j, step in enumerate((1, -1)):
            d_start(level3(p, here[o[2]], core), p * NS + j, peer(o[2], step))
        to_sibling(p, here[o[2]], None, 0)

    def stage3(p):
        o = parts[p][0]
        for j, step in enumerate((1, -1)):
            at = shifted(o[2], -step)
            d_wait(level3(p, at, core), p * NS + j)
            d_start(level3(p, at, core, j), p * NS + 2 + j, peer(o[2], step))
            to_sibling(p, at, None, 1 + j)

    def stage4(p):
        o = parts[p][0]
        for j in range(2):
            at = shifted(o[2], 2)
            d_wait(level3(p, at, core, j), p * NS + 2 + j)
            to_sibling(p, at, j, 3 + j)

    def c_start():
        for p in range(8):
            pltpu.make_async_copy(c_hbm.at[p], cbuf.at[p], c_sem.at[p]).start()

    def t_gather(p):
        pltpu.make_async_copy(rbuf.at[:, p], rbuf.at[:, p], t_recv.at[p]).wait()
        if opt["S1"]:
            for t in range(2):
                for kk in range(2):
                    both = rbuf[:, p, (t * 2 + kk) * 16:(t * 2 + kk + 1) * 16, :].astype(F32).reshape(16, 2, 8, 128)
                    for h in range(2):
                        tl[t, pl.ds(pl.multiple_of(p * 128, 128), 128), pl.ds((kk * 2 + h) * 128, 128)] = both[:, h].reshape(128, 128).astype(BF16)

    def lam_rows(p, lam, cols):
        o = parts[p][0]
        pos = {"z": lam // 4, "x": pl.ds(lax.rem(lam, 2) * 2, 2), "y": slice(None)}
        v = dparts[p][pos[o[2]], lax.rem(lam // 2, 2), pos[o[1]], pos[o[0]], :, cols]
        if o.index("y") > o.index("x"):
            v = jnp.swapaxes(v, 0, 1)
        return v.reshape(128, v.shape[-1])

    def step1():
        for p in ps:
            while sib_wait[p]:
                d_wait(*sib_wait[p].pop(0))

        @pl.loop(0, 8 // pg)
        def _(g):
            for q in range(pg):
                t_gather(g * pg + q)
            if not opt["S1"]:
                return

            for t in range(2):
                lams = [lam_ref[t, k] for k in range(4)]
                lhs = tl[t, pl.ds(pl.multiple_of(g * pg * 128, pg * 128), pg * 128)]
                for p in ps:
                    _, first, width = parts[p]
                    for start in range(0, width, 512):
                        nc = min(512, width - start)
                        rhs = jnp.concatenate([lam_rows(p, lam, pl.ds(start, nc)) for lam in lams], axis=0)
                        res = jnp.dot(lhs, rhs, preferred_element_type=F32).astype(BF16)
                        for q in range(pg):
                            for h in range(nc // 128):
                                prod[g * pg + q, (first + start) // 128 + h, :, pl.ds(t * 128, 128)] = (
                                    res[q * 128:(q + 1) * 128, h * 128:(h + 1) * 128].T)

    acts = {"1": stage1, "1b": stage1b, "2": stage2, "3": stage3, "4": stage4, "T": t_start, "S": step1, "C": c_start}
    used = set(opt["sched"])
    for name, *arg in opt["sched"]:
        acts[name](*arg)
    for p in ps:
        if ("1b", p) not in used:
            own_d[p].wait()
    if ("C",) in used:
        for p in range(8):
            pltpu.make_async_copy(c_hbm.at[p], cbuf.at[p], c_sem.at[p]).wait()

    def step2(nu):
        if not opt["S2"]:
            return jnp.zeros((128, 256), F32)
        sigs = [sig_ref[k, nu] for k in range(4)]
        lhs = jnp.concatenate([cbuf[p, nu, k] for p in range(8) for k in range(4)], axis=1)
        rhs = jnp.concatenate([prod[p, s] for p in range(8) for s in sigs], axis=0)
        return jnp.dot(lhs, rhs, preferred_element_type=F32)

    def spot(dx, dy):
        return lax.rem(x + dx + 4, 4) * 4 + lax.rem(y + dy + 4, 4)

    def mid_copy(s, nu, slot, dst):
        return pltpu.make_async_remote_copy(src_ref=kbf.at[nu], dst_ref=kmid.at[slot], send_sem=k_send.at[s], recv_sem=m_recv.at[slot],
                                            device_id=(r, dst), device_id_type=MESH)

    def own_copy(src_ref, s, dst, src):
        return pltpu.make_async_remote_copy(src_ref=src_ref, dst_ref=krecv.at[src], send_sem=k_send.at[s], recv_sem=k_recv.at[src],
                                            device_id=(r, dst), device_id_type=MESH)

    FIRST = 7

    def send(i, dx, dy, nu):
        @pl.when((i < 4) & (dx != 0))
        def _():
            mid_copy(i, nu, dx - 1, spot(dx, 0)).start()

        @pl.when((i >= 4) & (i < FIRST) & (dy != 0))
        def _():
            mid_copy(i, nu, 3 + dy // 2, spot(0, dy)).start()

        @pl.when((i >= FIRST) & (i < 15))
        def _():
            own_copy(kbf.at[nu], i, nu, c).start()

        @pl.when(i == opt["mid"])
        def _():
            for slot in range(5):
                pltpu.make_async_copy(kmid.at[slot], kmid.at[slot], m_recv.at[slot]).wait()
            for j, (slots, at) in enumerate((((0, 1, 2), spot(0, 2)), ((3, 4), spot(2, 0)))):
                tot = kbf[at].astype(F32)
                for slot in slots:
                    tot += kmid[slot].astype(F32)
                ksum[j] = tot.astype(BF16)
                own_copy(ksum.at[j], 16 + j, at, c).start()

    def two_nus(i, carry):
        cx, cy = carry
        at = [(cx % 4, cy % 4), (cx // 4 % 4, cy // 4 % 4)]
        nus = [spot(*v) for v in at]
        accs = [step2(nu) for nu in nus]
        for nu, acc in zip(nus, accs):
            kbf[nu] = acc.astype(BF16)
        if opt["K"]:
            for j in range(2):
                send(2 * i + j, *at[j], nus[j])

        @pl.when(i == 7)
        def _():
            out_ref[...] = accs[1]

        return cx // 16, cy // 16

    SEQ = ((1, 2), (2, 2), (3, 2), (0, 2), (2, 1), (2, 3), (2, 0), (1, 1), (3, 3), (1, 3), (3, 1), (1, 0), (0, 1), (3, 0), (0, 3))
    lax.fori_loop(0, 8, two_nus, tuple(jnp.int32(sum(v[a] * 4**i for i, v in enumerate(SEQ))) for a in range(2)))

    for cp in started:
        cp.wait_send()
    for p in range(8):
        if any(u[0] == "T" for u in used):
            pltpu.make_async_copy(rbuf.at[pl.ds(0, 15), p], rbuf.at[pl.ds(0, 15), p], t_send.at[p]).wait()

    if opt["K"]:
        last = SEQ[FIRST:] + ((0, 2), (2, 0))
        for dx, dy in last:
            src = spot(-dx, -dy)
            own_copy(ksum.at[0], 0, c, src).wait_recv()
            out_ref[...] += krecv[src].astype(F32)
        for i, (dx, dy) in enumerate(SEQ):
            if (dx, dy) not in ((0, 2), (2, 0)):
                pltpu.make_async_copy(kbf.at[0], kbf.at[0], k_send.at[i]).wait()
        for j in range(2):
            pltpu.make_async_copy(kbf.at[0], kbf.at[0], k_send.at[16 + j]).wait()


def per_device(opt, tensor_blocks, density, coef, lam_list, sig_list):
    parts = opt["parts"]
    return pl.pallas_call(
        functools.partial(kernel, opt),
        out_shape=pltpu.VMEM((128, 256), F32),
        in_specs=[pl.BlockSpec(memory_space=pltpu.SMEM)] * 2 + [pl.BlockSpec(memory_space=pl.ANY)] * 3,
        out_specs=pl.BlockSpec(memory_space=pltpu.VMEM),
        scratch_shapes=[
            pltpu.VMEM((8, 16, 4, 128, 128), BF16),
            pltpu.VMEM((16, 8, 64, 128), BF16),
            pltpu.VMEM((2, 1024, 512), BF16),
            pltpu.VMEM((8, 16, 128, 256), BF16),
            pltpu.VMEM((16, 128, 256), BF16),
            pltpu.VMEM((16, 128, 256), BF16),
            pltpu.SemaphoreType.DMA((16 * len(parts),)),
            pltpu.SemaphoreType.DMA((16 * len(parts),)),
            pltpu.SemaphoreType.DMA((8,)),
            pltpu.SemaphoreType.DMA((8,)),
            pltpu.SemaphoreType.DMA((18,)),
            pltpu.SemaphoreType.DMA((16,)),
            pltpu.SemaphoreType.DMA((len(parts),)),
            pltpu.SemaphoreType.DMA((8,)),
            pltpu.VMEM((5, 128, 256), BF16),
            pltpu.VMEM((2, 128, 256), BF16),
            pltpu.SemaphoreType.DMA((5,)),
        ] + [pltpu.VMEM((4, 2, 4, 4, 16, width), BF16) for _, _, width in parts],
        compiler_params=pltpu.CompilerParams(collective_id=0, has_side_effects=True, vmem_limit_bytes=60 * 2**20),
        cost_estimate=pl.CostEstimate(flops=2**33, bytes_accessed=20 * 2**20, transcendentals=0),
    )(lam_list, sig_list.T, tensor_blocks.reshape(128, 64, 128), density, coef)


def solution(mesh, **kw):
    in_specs = (
        P(None, "row", None, "col", None),
        P(("row", "col"), None),
        P("col", None, None, None, None),
        P("row", None),
        P(),
    )
    return jax.shard_map(functools.partial(per_device, {**OPT, **kw}), mesh=mesh, in_specs=in_specs, out_specs=P("col", "row"), check_vma=False)
```

```python
import functools

import jax
import jax.numpy as jnp
from jax import lax
from jax.experimental import pallas as pl
from jax.experimental.pallas import tpu as pltpu
from jax.sharding import PartitionSpec as P

MESH = pl.DeviceIdType.MESH
F32, BF16 = jnp.float32, jnp.bfloat16
PARTS = (("xyz", 0, 768), ("yxz", 768, 768), ("zxy", 1536, 256), ("zyx", 1792, 256))
ORDER = tuple(((i + i // 4) % 4, i % 4) for i in range(1, 16))
SCHED = (("1", 0), ("1", 1), ("1", 2), ("1", 3), ("1b", 0), ("1b", 1), ("1b", 2), ("1b", 3), ("T", 0, 2), ("2", 0), ("2", 1), ("2", 2), ("2", 3),
         ("T", 2, 4), ("C",), ("3", 2), ("3", 3), ("T", 4, 8), ("3", 0), ("3", 1), ("4", 2), ("4", 3), ("G",), ("4", 0), ("4", 1), ("S",))
OPT = dict(S1=True, S2=True, K=True, pg=4, parts=PARTS, sched=SCHED, order=ORDER, bar=False, mid=13)


def kernel(opt, lam_ref, sig_ref, t_hbm, d_hbm, c_hbm, out_ref, cbuf, rbuf, tl, prod, kbf, krecv,
           d_send, d_recv, t_send, t_recv, k_send, k_recv, loc_sem, c_sem, kmid, ksum, m_recv, *dparts):
    parts, pg = opt["parts"], opt["pg"]
    r, c = lax.axis_index("row"), lax.axis_index("col")
    z, core, x, y = r // 2, r % 2, c // 4, c % 4
    here = {"x": x, "y": y, "z": z}

    def peer(axis, step):
        n = lax.rem(here[axis] + step + 4, 4)
        if axis == "z":
            return (n * 2 + core, c)
        return (r, n * 4 + y) if axis == "x" else (r, x * 4 + n)

    sibling = (r + 1 - 2 * core, c)

    own_d = [pltpu.make_async_copy(d_hbm.at[:, pl.ds(first, width)],
                                   dparts[p].at[here[order[2]], core, here[order[1]], here[order[0]]], loc_sem.at[p])
             for p, (order, first, width) in enumerate(parts)]
    for cp in own_d:
        cp.start()
    for p in range(8):
        pltpu.make_async_copy(t_hbm.at[c * 8 + p], rbuf.at[c, p], t_recv.at[p]).start()

    barrier = pltpu.get_barrier_semaphore()

    def greet(dev):
        pl.semaphore_signal(barrier, inc=1, device_id=dev, device_id_type=MESH)

    for axis in "xyz":
        for step in (1, 2, 3):
            greet(peer(axis, step))
    greet(sibling)
    if opt["bar"]:
        for dx in (1, 2, 3):
            for dy in (1, 2, 3):
                greet((r, lax.rem(x + dx, 4) * 4 + lax.rem(y + dy, 4)))
    pl.semaphore_wait(barrier, 19 if opt["bar"] else 10)

    def t_start(first, last):
        @pl.loop(first, last)
        def _(p):
            for dx, dy in opt["order"]:
                dst = lax.rem(x + dx, 4) * 4 + lax.rem(y + dy, 4)
                pltpu.make_async_remote_copy(src_ref=t_hbm.at[dst * 8 + p], dst_ref=rbuf.at[c, p], send_sem=t_send.at[p], recv_sem=t_recv.at[p],
                                             device_id=(r, dst), device_id_type=MESH).start()

    started = []
    sib_wait = {p: [] for p in range(len(parts))}
    NS = 16

    def d_start(ref, s, dev):
        cp = pltpu.make_async_remote_copy(src_ref=ref, dst_ref=ref, send_sem=d_send.at[s], recv_sem=d_recv.at[s],
                                          device_id=dev, device_id_type=MESH)
        cp.start()
        started.append(cp)

    def d_wait(ref, s):
        pltpu.make_async_copy(ref, ref, d_recv.at[s]).wait()

    def shifted(axis, step):
        return lax.rem(here[axis] + step + 4, 4)

    def level1(p, a, core_at=core):
        o = parts[p][0]
        return dparts[p].at[here[o[2]], core_at, here[o[1]], a]

    def level2(p, a):
        o = parts[p][0]
        return dparts[p].at[here[o[2]], core, a]

    def level3(p, a, core_at, half=None):
        ref = dparts[p].at[a, core_at]
        return ref if half is None else ref.at[pl.ds(half * 2, 2)]

    def to_sibling(p, a, half, j):
        d_start(level3(p, a, core, half), p * NS + 4 + j, sibling)
        sib_wait[p].append((level3(p, a, 1 - core, half), p * NS + 4 + j))

    STEPS = (1, -1, 2)
    ps = range(len(parts))

    def stage1(p):
        o, first, width = parts[p]
        for j, step in enumerate(STEPS):
            s = p * NS + 10 + j
            cp = pltpu.make_async_remote_copy(src_ref=d_hbm.at[:, pl.ds(first, width)], dst_ref=level1(p, here[o[0]]), send_sem=d_send.at[s],
                                              recv_sem=d_recv.at[s], device_id=peer(o[0], step), device_id_type=MESH)
            cp.start()
            started.append(cp)

    def stage1b(p):
        o = parts[p][0]
        own_d[p].wait()
        for j, step in enumerate(STEPS):
            d_wait(level1(p, shifted(o[0], -step)), p * NS + 10 + j)
        for j, step in enumerate(STEPS):
            d_start(level2(p, here[o[1]]), p * NS + 13 + j, peer(o[1], step))

    def stage2(p):
        o = parts[p][0]
        for j, step in enumerate(STEPS):
            d_wait(level2(p, shifted(o[1], -step)), p * NS + 13 + j)
        for j, step in enumerate((1, -1)):
            d_start(level3(p, here[o[2]], core), p * NS + j, peer(o[2], step))
        to_sibling(p, here[o[2]], None, 0)

    def stage3(p):
        o = parts[p][0]
        for j, step in enumerate((1, -1)):
            at = shifted(o[2], -step)
            d_wait(level3(p, at, core), p * NS + j)
            d_start(level3(p, at, core, j), p * NS + 2 + j, peer(o[2], step))
            to_sibling(p, at, None, 1 + j)

    def stage4(p):
        o = parts[p][0]
        for j in range(2):
            at = shifted(o[2], 2)
            d_wait(level3(p, at, core, j), p * NS + 2 + j)
            to_sibling(p, at, j, 3 + j)

    def c_start():
        for p in range(8):
            pltpu.make_async_copy(c_hbm.at[p], cbuf.at[p], c_sem.at[p]).start()

    def t_gather(p):
        pltpu.make_async_copy(rbuf.at[:, p], rbuf.at[:, p], t_recv.at[p]).wait()
        if opt["S1"]:
            for t in range(2):
                for kk in range(2):
                    both = rbuf[:, p, (t * 2 + kk) * 16:(t * 2 + kk + 1) * 16, :].astype(F32).reshape(16, 2, 8, 128)
                    for h in range(2):
                        tl[t, pl.ds(pl.multiple_of(p * 128, 128), 128), pl.ds((kk * 2 + h) * 128, 128)] = both[:, h].reshape(128, 128).astype(BF16)

    def lam_rows(p, lam, cols):
        o = parts[p][0]
        pos = {"z": lam // 4, "x": pl.ds(lax.rem(lam, 2) * 2, 2), "y": slice(None)}
        v = dparts[p][pos[o[2]], lax.rem(lam // 2, 2), pos[o[1]], pos[o[0]], :, cols]
        if o.index("y") > o.index("x"):
            v = jnp.swapaxes(v, 0, 1)
        return v.reshape(128, v.shape[-1])

    def step1():
        for p in ps:
            while sib_wait[p]:
                d_wait(*sib_wait[p].pop(0))

        @pl.loop(0, 8 // pg)
        def _(g):
            @pl.when(g > 0)
            def _():
                for q in range(pg):
                    t_gather(g * pg + q)

            if not opt["S1"]:
                return

            for t in range(2):
                lams = [lam_ref[t, k] for k in range(4)]
                lhs = tl[t, pl.ds(pl.multiple_of(g * pg * 128, pg * 128), pg * 128)]
                for p in ps:
                    _, first, width = parts[p]
                    for start in range(0, width, 512):
                        nc = min(512, width - start)
                        rhs = jnp.concatenate([lam_rows(p, lam, pl.ds(start, nc)) for lam in lams], axis=0)
                        res = jnp.dot(lhs, rhs, preferred_element_type=F32).astype(BF16)
                        for q in range(pg):
                            for h in range(nc // 128):
                                prod[g * pg + q, (first + start) // 128 + h, :, pl.ds(t * 128, 128)] = (
                                    res[q * 128:(q + 1) * 128, h * 128:(h + 1) * 128].T)

    def gather_first():
        pl.loop(0, pg)(t_gather)

    acts = {"G": gather_first, "1": stage1, "1b": stage1b, "2": stage2, "3": stage3, "4": stage4, "T": t_start, "S": step1, "C": c_start}
    used = set(opt["sched"])
    for name, *arg in opt["sched"]:
        acts[name](*arg)
    for p in ps:
        if ("1b", p) not in used:
            own_d[p].wait()
    if ("C",) in used:
        for p in range(8):
            pltpu.make_async_copy(c_hbm.at[p], cbuf.at[p], c_sem.at[p]).wait()

    def step2(nu):
        if not opt["S2"]:
            return jnp.zeros((128, 256), F32)
        sigs = [sig_ref[k, nu] for k in range(4)]
        lhs = jnp.concatenate([cbuf[p, nu, k] for p in range(8) for k in range(4)], axis=1)
        rhs = jnp.concatenate([prod[p, s] for p in range(8) for s in sigs], axis=0)
        return jnp.dot(lhs, rhs, preferred_element_type=F32)

    def spot(dx, dy):
        return lax.rem(x + dx + 4, 4) * 4 + lax.rem(y + dy + 4, 4)

    def mid_copy(s, nu, slot, dst):
        return pltpu.make_async_remote_copy(src_ref=kbf.at[nu], dst_ref=kmid.at[slot], send_sem=k_send.at[s], recv_sem=m_recv.at[slot],
                                            device_id=(r, dst), device_id_type=MESH)

    def own_copy(src_ref, s, dst, src):
        return pltpu.make_async_remote_copy(src_ref=src_ref, dst_ref=krecv.at[src], send_sem=k_send.at[s], recv_sem=k_recv.at[src],
                                            device_id=(r, dst), device_id_type=MESH)

    FIRST = 7

    def send(i, dx, dy, nu):
        @pl.when((i < 4) & (dx != 0))
        def _():
            mid_copy(i, nu, dx - 1, spot(dx, 0)).start()

        @pl.when((i >= 4) & (i < FIRST) & (dy != 0))
        def _():
            mid_copy(i, nu, 3 + dy // 2, spot(0, dy)).start()

        @pl.when((i >= FIRST) & (i < 15))
        def _():
            own_copy(kbf.at[nu], i, nu, c).start()

        @pl.when(i == opt["mid"])
        def _():
            for slot in range(5):
                pltpu.make_async_copy(kmid.at[slot], kmid.at[slot], m_recv.at[slot]).wait()
            for j, (slots, at) in enumerate((((0, 1, 2), spot(0, 2)), ((3, 4), spot(2, 0)))):
                tot = kbf[at].astype(F32)
                for slot in slots:
                    tot += kmid[slot].astype(F32)
                ksum[j] = tot.astype(BF16)
                own_copy(ksum.at[j], 16 + j, at, c).start()

    def two_nus(i, carry):
        cx, cy = carry
        at = [(cx % 4, cy % 4), (cx // 4 % 4, cy // 4 % 4)]
        nus = [spot(*v) for v in at]
        accs = [step2(nu) for nu in nus]
        for nu, acc in zip(nus, accs):
            kbf[nu] = acc.astype(BF16)
        if opt["K"]:
            for j in range(2):
                send(2 * i + j, *at[j], nus[j])

        @pl.when(i == 7)
        def _():
            out_ref[...] = accs[1]

        return cx // 16, cy // 16

    SEQ = ((1, 2), (2, 2), (3, 2), (0, 2), (2, 1), (2, 3), (2, 0), (1, 1), (3, 3), (1, 3), (3, 1), (1, 0), (0, 1), (3, 0), (0, 3))
    lax.fori_loop(0, 8, two_nus, tuple(jnp.int32(sum(v[a] * 4**i for i, v in enumerate(SEQ))) for a in range(2)))

    for cp in started:
        cp.wait_send()
    for p in range(8):
        if any(u[0] == "T" for u in used):
            pltpu.make_async_copy(rbuf.at[pl.ds(0, 15), p], rbuf.at[pl.ds(0, 15), p], t_send.at[p]).wait()

    if opt["K"]:
        last = SEQ[FIRST:] + ((0, 2), (2, 0))
        for dx, dy in last:
            src = spot(-dx, -dy)
            own_copy(ksum.at[0], 0, c, src).wait_recv()
            out_ref[...] += krecv[src].astype(F32)
        for i, (dx, dy) in enumerate(SEQ):
            if (dx, dy) not in ((0, 2), (2, 0)):
                pltpu.make_async_copy(kbf.at[0], kbf.at[0], k_send.at[i]).wait()
        for j in range(2):
            pltpu.make_async_copy(kbf.at[0], kbf.at[0], k_send.at[16 + j]).wait()


def per_device(opt, tensor_blocks, density, coef, lam_list, sig_list):
    parts = opt["parts"]
    return pl.pallas_call(
        functools.partial(kernel, opt),
        out_shape=pltpu.VMEM((128, 256), F32),
        in_specs=[pl.BlockSpec(memory_space=pltpu.SMEM)] * 2 + [pl.BlockSpec(memory_space=pl.ANY)] * 3,
        out_specs=pl.BlockSpec(memory_space=pltpu.VMEM),
        scratch_shapes=[
            pltpu.VMEM((8, 16, 4, 128, 128), BF16),
            pltpu.VMEM((16, 8, 64, 128), BF16),
            pltpu.VMEM((2, 1024, 512), BF16),
            pltpu.VMEM((8, 16, 128, 256), BF16),
            pltpu.VMEM((16, 128, 256), BF16),
            pltpu.VMEM((16, 128, 256), BF16),
            pltpu.SemaphoreType.DMA((16 * len(parts),)),
            pltpu.SemaphoreType.DMA((16 * len(parts),)),
            pltpu.SemaphoreType.DMA((8,)),
            pltpu.SemaphoreType.DMA((8,)),
            pltpu.SemaphoreType.DMA((18,)),
            pltpu.SemaphoreType.DMA((16,)),
            pltpu.SemaphoreType.DMA((len(parts),)),
            pltpu.SemaphoreType.DMA((8,)),
            pltpu.VMEM((5, 128, 256), BF16),
            pltpu.VMEM((2, 128, 256), BF16),
            pltpu.SemaphoreType.DMA((5,)),
        ] + [pltpu.VMEM((4, 2, 4, 4, 16, width), BF16) for _, _, width in parts],
        compiler_params=pltpu.CompilerParams(collective_id=0, has_side_effects=True, vmem_limit_bytes=60 * 2**20),
        cost_estimate=pl.CostEstimate(flops=2**33, bytes_accessed=20 * 2**20, transcendentals=0),
    )(lam_list, sig_list.T, tensor_blocks.reshape(128, 64, 128), density, coef)


def solution(mesh, **kw):
    in_specs = (
        P(None, "row", None, "col", None),
        P(("row", "col"), None),
        P("col", None, None, None, None),
        P("row", None),
        P(),
    )
    return jax.shard_map(functools.partial(per_device, {**OPT, **kw}), mesh=mesh, in_specs=in_specs, out_specs=P("col", "row"), check_vma=False)
```
